128 devices in a mesh: tm: 128 (over z, y, x, core).
Axes of the slice: x: 4, y: 4, z: 4, core: 2. Of those that a mesh axis runs over, the one named last changes fastest.
Arguments:
- wrapped: float32 [16384, 3, 512], P('tm'), may hold values from 0 to 1, as said below
- crossings: int32 [16384, 3, 512], P('tm'), may hold values from -1 to 1, as said below
- box_size: float32 [3], replicated, may hold values from 4 to 12
Outputs:
- msd: float32 [512, 128], P('tm')
The draws below stay inside these ranges and needn't reach their ends.
Inputs may be any that keep to these rules, and one draw needn't show every extreme that they name: `wrapped`: scaled coordinates within the unit cell. per-frame crossings, one of -1, 0, 1; most entries are 0.
All inputs are finite; a program needn't handle non-finite values.
Results may differ from the reference program's by a relative error of at most 0.0003.
Values sent between devices are 32-bit elements; how exact they have to be, the bound alone decides.
No kernel may reach another device: no remote copies, remote signals or barrier semaphores. Data moves between devices by JAX's collectives and lax.ppermute only.
A program may use at most 64 MiB of HBM per device.

```python
import math
import jax
import jax.numpy as jnp
from jax import lax

ATOMS = 512
LAGS = 128
NT = 16384


def draw_wrapped(key, part):
    base_key, jitter_key = jax.random.split(jax.random.fold_in(key, 11))
    base = jax.random.uniform(base_key, (1, 3, ATOMS), jnp.float32)
    jitter = 0.08 * jax.random.normal(jitter_key, (NT, 3, ATOMS), jnp.float32)
    return jnp.mod(base + jitter, 1.0)


def draw_crossings(key, part):
    rolls = jax.random.randint(jax.random.fold_in(key, 23), (NT, 3, ATOMS), 0, 256, dtype=jnp.int32)
    upward = jnp.where(rolls == 0, 1, 0).astype(jnp.int32)
    downward = jnp.where(rolls == 255, 1, 0).astype(jnp.int32)
    return upward - downward


def setup_inputs(seed: int = 0) -> dict:
    key_list = jax.random.split(jax.random.key(seed), 4)
    wrapped = draw_wrapped(jax.random.fold_in(key_list[3], 71), 0)
    crossings = draw_crossings(jax.random.fold_in(key_list[3], 71), 0)
    box_size = jnp.clip(jnp.exp(jax.random.uniform(key_list[2], (3,), jnp.float32, math.log(4.0), math.log(12.0))), 4.0, 12.0)
    return {"wrapped": wrapped, "crossings": crossings, "box_size": box_size}


def reference(wrapped, crossings, box_size):
    image = jnp.cumsum(crossings, axis=0)
    unwrapped = (wrapped + image.astype(jnp.float32)) * box_size[None, :, None]
    total_frames = unwrapped.shape[0]
    atom_count = unwrapped.shape[2]
    frame_ids = jnp.arange(total_frames, dtype=jnp.int32)

    def per_block(first_atom):
        block = lax.dynamic_slice_in_dim(unwrapped, first_atom, 128, 2)
        extended = jnp.concatenate([block, jnp.zeros((LAGS, 3, 128), jnp.float32)], axis=0)

        def per_lag(lag_step):
            window = lax.dynamic_slice_in_dim(extended, lag_step, total_frames, 0)
            moved = window - block
            squares = jnp.sum(moved * moved, axis=1)
            in_range = (frame_ids + lag_step) < total_frames
            return jnp.sum(jnp.where(in_range[:, None], squares, jnp.float32(0.0)), axis=0)

        return lax.map(per_lag, jnp.arange(LAGS, dtype=jnp.int32))

    parts = lax.map(per_block, jnp.arange(atom_count // 128, dtype=jnp.int32) * 128)
    lag_sum = jnp.transpose(parts, (1, 0, 2)).reshape(LAGS, atom_count)
    divisor = (total_frames - jnp.arange(LAGS, dtype=jnp.int32)).astype(jnp.float32)
    return (lag_sum / divisor[:, None]).T
```

```python
import functools

import jax
import jax.numpy as jnp
import numpy as np
from jax import lax
from jax.experimental import pallas as pl
from jax.experimental.pallas import tpu as pltpu
from jax.sharding import PartitionSpec as P

LAGS = 128
FRAMES = 128
CHUNKS = 128
ROWS = 16
GROUP = 8
VMEM = 48 * 1024 * 1024


def tables():
    t = np.arange(FRAMES)[:, None].astype(np.float64)
    f = np.arange(FRAMES)[None, :].astype(np.float64)
    angle = 2.0 * np.pi * t * f / 256.0
    alternate = 1.0 - 2.0 * (np.arange(128) % 2)
    imaginary = -np.sin(angle)
    imaginary[:, 0] = alternate
    forward = np.concatenate([np.cos(angle), imaginary], axis=1)
    high = forward.astype(jnp.bfloat16)
    low = (forward - high.astype(np.float64)).astype(jnp.bfloat16)

    weight = np.full((128, 1), 2.0 / 256.0)
    weight[0] = 1.0 / 256.0
    sign = alternate[:, None]
    cosine = np.cos(angle)
    same = 2.0 * weight * (1.0 - cosine)
    same[0] = 2.0 / 256.0 * (1.0 - alternate)
    real = -2.0 * weight * sign * cosine
    imag = 2.0 * weight * sign * np.sin(angle)
    imag[0] = -2.0 / 256.0 * alternate
    j = np.arange(128)[:, None]
    k = np.arange(128)[None, :]
    head = (j < k).astype(np.float64)
    tail = (j > 127 - k).astype(np.float64)
    backward = np.concatenate([same, real, imag, head, tail]).astype(np.float32)
    return high, low, backward


def pre_kernel(wrapped_ref, crossings_ref, out_ref):
    row = lax.broadcasted_iota(jnp.int32, (FRAMES, FRAMES), 0)
    col = lax.broadcasted_iota(jnp.int32, (FRAMES, FRAMES), 1)
    lower = jnp.where(col <= row, 1.0, 0.0).astype(jnp.bfloat16)
    notes = []
    for c in range(3):
        steps = crossings_ref[c].astype(jnp.float32).astype(jnp.bfloat16)
        counts = jnp.dot(lower, steps, preferred_element_type=jnp.float32)
        value = wrapped_ref[c] + counts
        mean = jnp.sum(value, axis=0, keepdims=True) * (1.0 / FRAMES)
        out_ref[:, 4 * c : 4 * c + 4, :] = (value - mean).T.reshape(CHUNKS, 4, FRAMES)
        notes += [mean, counts[FRAMES - 1 : FRAMES] - mean]
    notes.append(jnp.zeros((2, 512), jnp.float32))
    out_ref[:, 12:16, 0:8] = jnp.concatenate(notes, axis=0).T.reshape(CHUNKS, 4, 8)


def post_kernel(x_ref, high_ref, low_ref, back_ref, box_ref, out_ref, spec_ref, shift_ref):
    high = high_ref[...]
    low = low_ref[...]
    for g in range(CHUNKS // 16):
        block = x_ref[16 * g : 16 * g + 16].reshape(256, 128)
        top = block.astype(jnp.bfloat16)
        rest = (block - top.astype(jnp.float32)).astype(jnp.bfloat16)
        spec = jnp.dot(top, high, preferred_element_type=jnp.float32)
        spec += jnp.dot(top, low, preferred_element_type=jnp.float32)
        spec += jnp.dot(rest, high, preferred_element_type=jnp.float32)
        spec_ref[16 * g : 16 * g + 16] = spec.reshape(16, ROWS, 256)
    spec_ref[CHUNKS] = jnp.zeros((ROWS, 256), jnp.float32)

    for c in range(3):
        mean = x_ref[1:CHUNKS, 12:16, 2 * c : 2 * c + 1]
        gap = x_ref[0 : CHUNKS - 1, 12:16, 2 * c + 1 : 2 * c + 2] + mean
        shift_ref[0 : CHUNKS - 1, 4 * c : 4 * c + 4, :] = jnp.broadcast_to(
            gap, (CHUNKS - 1, 4, 128)
        )
    shift_ref[CHUNKS - 1] = jnp.zeros((ROWS, 128), jnp.float32)

    zero = jnp.zeros((ROWS, 128), jnp.float32)

    def one(d, acc):
        same_r, same_i, rr, ii, ri, ir, za, zb, dd = acc
        here_r = spec_ref[d, :, 0:128]
        here_i = spec_ref[d, :, 128:256]
        next_r = spec_ref[d + 1, :, 0:128]
        next_i = spec_ref[d + 1, :, 128:256]
        gap = shift_ref[d]
        return (
            same_r + here_r * here_r,
            same_i + here_i * here_i,
            rr + here_r * next_r,
            ii + here_i * next_i,
            ri + here_r * next_i,
            ir + here_i * next_r,
            za + gap * x_ref[d],
            zb + gap * x_ref[jnp.minimum(d + 1, CHUNKS - 1)],
            dd + gap * gap,
        )

    def body(g, acc):
        for u in range(GROUP):
            acc = one(g * GROUP + u, acc)
        return acc

    acc = lax.fori_loop(0, CHUNKS // GROUP, body, (zero,) * 9)
    same_r, same_i, rr, ii, ri, ir, za, zb, dd = acc
    lane = lax.broadcasted_iota(jnp.int32, (ROWS, 128), 1)
    first = lane == 0
    first_chunk = x_ref[0]
    last_chunk = x_ref[CHUNKS - 1]
    parts = jnp.concatenate(
        [
            same_i + jnp.where(first, 0.0, same_r),
            rr + jnp.where(first, 0.0, ii),
            jnp.where(first, ii, ri - ir),
            2.0 * zb - first_chunk * first_chunk,
            -2.0 * za - last_chunk * last_chunk,
        ],
        axis=1,
    )
    sums = jnp.dot(
        parts, back_ref[...], precision=lax.Precision.HIGHEST, preferred_element_type=jnp.float32
    )
    lags = lane.astype(jnp.float32)
    sums = sums + dd * lags
    total = jnp.zeros((4, 128), jnp.float32)
    for c in range(3):
        total = total + sums[4 * c : 4 * c + 4] * (box_ref[c] * box_ref[c])
    out_ref[...] = total / (FRAMES * CHUNKS - lags[0:4])


def on_device(wrapped, crossings, box_size):
    high, low, backward = tables()
    params = pltpu.CompilerParams(vmem_limit_bytes=VMEM)
    whole = pl.BlockSpec(memory_space=pltpu.VMEM)
    blocks = pl.pallas_call(
        pre_kernel,
        out_shape=jax.ShapeDtypeStruct((CHUNKS, ROWS, FRAMES), jnp.float32),
        in_specs=[whole, whole],
        out_specs=whole,
        compiler_params=params,
    )(jnp.transpose(wrapped, (1, 0, 2)), jnp.transpose(crossings, (1, 0, 2)))
    mine = lax.all_to_all(blocks, "tm", split_axis=0, concat_axis=0, tiled=True)
    return pl.pallas_call(
        post_kernel,
        out_shape=jax.ShapeDtypeStruct((4, LAGS), jnp.float32),
        in_specs=[whole, whole, whole, whole, pl.BlockSpec(memory_space=pltpu.SMEM)],
        out_specs=whole,
        scratch_shapes=[
            pltpu.VMEM((CHUNKS + 8, ROWS, 256), jnp.float32),
            pltpu.VMEM((CHUNKS, ROWS, 128), jnp.float32),
        ],
        compiler_params=params,
    )(mine, jnp.asarray(high), jnp.asarray(low), jnp.asarray(backward), box_size)


def solution(mesh):
    in_specs = (P("tm", None, None), P("tm", None, None), P())
    return jax.shard_map(
        on_device, mesh=mesh, in_specs=in_specs, out_specs=P("tm", None), check_vma=False
    )
```

```python
import jax
import jax.numpy as jnp
import numpy as np
from jax import lax
from jax.experimental import pallas as pl
from jax.experimental.pallas import tpu as pltpu
from jax.sharding import PartitionSpec as P

LAGS = 128
FRAMES = 128
CHUNKS = 128
ATOMS = 512
SENT = 13
ROWS = 16
PIECES = 2
VMEM = 48 * 1024 * 1024


def split(x):
    high = x.astype(jnp.bfloat16)
    low = (x - high.astype(x.dtype)).astype(jnp.bfloat16)
    return high, low


def tables():
    t = np.arange(FRAMES)[:, None].astype(np.float64)
    f = np.arange(FRAMES)[None, :].astype(np.float64)
    angle = 2.0 * np.pi * t * (f + 0.5) / 256.0
    forward = np.concatenate([np.cos(angle), -np.sin(angle)], axis=1)
    high, low = split(forward)
    forward = np.concatenate([high, high, low])

    turn = angle.T
    weight = 2.0 / 256.0
    sign = (1.0 - 2.0 * (np.arange(128) % 2))[:, None]
    same = 2.0 * weight * (1.0 - np.cos(turn))
    real = -2.0 * weight * sign * np.sin(turn)
    imag = -2.0 * weight * sign * np.cos(turn)
    j = np.arange(128)[:, None]
    k = np.arange(128)[None, :]
    head = (j < k).astype(np.float64)
    tail = (j > 127 - k).astype(np.float64)
    high, low = split(np.concatenate([same, real, imag, head, tail]))
    return forward, np.concatenate([high, low[:384]])


def pre_kernel(wrapped_hbm, crossings_hbm, out_ref, wrapped_ref, crossings_ref, sems):
    copies = []
    for c in range(3):
        for p in range(PIECES):
            rows = pl.ds(p * (FRAMES // PIECES), FRAMES // PIECES)
            for which, (src, dst) in enumerate(
                ((crossings_hbm, crossings_ref), (wrapped_hbm, wrapped_ref))
            ):
                copy = pltpu.make_async_copy(
                    src.at[c, rows], dst.at[c, rows], sems.at[(c * PIECES + p) * 2 + which]
                )
                copy.start()
                copies.append(copy)
    row = lax.broadcasted_iota(jnp.int32, (FRAMES, FRAMES), 0)
    col = lax.broadcasted_iota(jnp.int32, (FRAMES, FRAMES), 1)
    lower = jnp.where(col <= row, 1.0, 0.0).astype(jnp.bfloat16)
    own = lax.broadcasted_iota(jnp.int32, (4, ATOMS), 1) % 4 == lax.broadcasted_iota(
        jnp.int32, (4, ATOMS), 0
    )
    means, ends = [], []
    for c in range(3):
        for copy in copies[c * 2 * PIECES : (c + 1) * 2 * PIECES]:
            copy.wait()
        steps = crossings_ref[c].astype(jnp.float32).astype(jnp.bfloat16)
        counts = jnp.dot(lower, steps, preferred_element_type=jnp.float32)
        value = wrapped_ref[c] + counts
        mean = jnp.sum(value, axis=0, keepdims=True) * (1.0 / FRAMES)
        turned = (value - mean).T
        for d in range(CHUNKS):
            out_ref[SENT * d + 4 * c : SENT * d + 4 * c + 4, :] = turned[4 * d : 4 * d + 4]
        means.append(jnp.where(own, mean, 0.0))
        ends.append(jnp.where(own, counts[FRAMES - 1 : FRAMES] - mean, 0.0))
    blank = jnp.zeros((4, ATOMS), jnp.float32)
    notes = jnp.concatenate(means + [blank] + ends + [blank] * 25, axis=0)
    pick = jnp.where(
        lax.broadcasted_iota(jnp.int32, (CHUNKS, ATOMS), 1) // 4
        == lax.broadcasted_iota(jnp.int32, (CHUNKS, ATOMS), 0),
        1.0,
        0.0,
    ).astype(jnp.bfloat16)
    sent = jnp.zeros((CHUNKS, 128), jnp.float32)
    for _ in range(3):
        top = notes.astype(jnp.bfloat16)
        notes = notes - top.astype(jnp.float32)
        sent = sent + lax.dot_general(
            pick, top, (((1,), (1,)), ((), ())), preferred_element_type=jnp.float32
        )
    out_ref[pl.ds(SENT - 1, CHUNKS, stride=SENT), :] = sent


def post_kernel(x_ref, forward_ref, back_ref, box_ref, out_ref, wide_ref, real_ref, imag_ref):
    here = x_ref[pl.ds(SENT - 1, CHUNKS, stride=SENT), :]
    after = x_ref[pl.ds(2 * SENT - 1, CHUNKS - 1, stride=SENT), :]
    after = jnp.concatenate([after, jnp.zeros((1, 128), jnp.float32)], axis=0)
    ends = jnp.concatenate([here[:, 16:], here[:, :16]], axis=1)
    chunk = lax.broadcasted_iota(jnp.int32, (CHUNKS, 128), 0)
    gaps = jnp.where(chunk < CHUNKS - 1, after + ends, 0.0).T[0:ROWS]

    for d in range(CHUNKS):
        rows = ROWS if d < CHUNKS - 1 else SENT
        wide_ref[ROWS * d : ROWS * d + rows, :] = x_ref[SENT * d : SENT * d + rows, :]
    wide_ref[ROWS * CHUNKS - 3 : ROWS * CHUNKS, :] = jnp.zeros((3, 128), jnp.float32)
    for g in range(8):
        rows = slice(256 * g, 256 * g + 256)
        top, rest = split(wide_ref[rows, :])
        spec = jnp.dot(
            jnp.concatenate([top, rest, top], axis=1),
            forward_ref[...],
            preferred_element_type=jnp.float32,
        )
        real_ref[rows, :] = spec[:, :128]
        imag_ref[rows, :] = spec[:, 128:]

    zero = jnp.zeros((ROWS, 128), jnp.float32)
    same = both_r = both_i = za = zb = zero
    block = slice(0, ROWS)
    here_r, here_i, here_x = real_ref[block, :], imag_ref[block, :], wide_ref[block, :]
    for d in range(CHUNKS):
        same = same + (here_r * here_r + here_i * here_i)
        if d == CHUNKS - 1:
            break
        block = slice(ROWS * (d + 1), ROWS * (d + 2))
        next_r, next_i, next_x = real_ref[block, :], imag_ref[block, :], wide_ref[block, :]
        both_r = both_r + (here_r * next_r + here_i * next_i)
        both_i = both_i + (here_r * next_i - here_i * next_r)
        gap = jnp.broadcast_to(gaps[:, d : d + 1], (ROWS, 128))
        za = za + gap * here_x
        zb = zb + gap * next_x
        here_r, here_i, here_x = next_r, next_i, next_x
    first_x = wide_ref[0:ROWS, :]

    parts = jnp.concatenate(
        [
            same,
            both_r,
            both_i,
            2.0 * zb - first_x * first_x,
            -2.0 * za - here_x * here_x,
        ],
        axis=1,
    )
    top, rest = split(parts)
    sums = jnp.dot(top, back_ref[0:640, :], preferred_element_type=jnp.float32)
    sums += jnp.dot(rest, back_ref[0:640, :], preferred_element_type=jnp.float32)
    sums += jnp.dot(top[:, :384], back_ref[640:1024, :], preferred_element_type=jnp.float32)
    lags = lax.broadcasted_iota(jnp.int32, (ROWS, 128), 1).astype(jnp.float32)
    sums = sums + jnp.sum(gaps * gaps, axis=1, keepdims=True) * lags
    total = jnp.zeros((4, 128), jnp.float32)
    for c in range(3):
        total = total + sums[4 * c : 4 * c + 4] * (box_ref[c] * box_ref[c])
    out_ref[...] = total / (FRAMES * CHUNKS - lags[0:4])


def on_device(wrapped, crossings, box_size):
    forward, backward = tables()
    params = pltpu.CompilerParams(vmem_limit_bytes=VMEM)
    whole = pl.BlockSpec(memory_space=pltpu.VMEM)
    apart = pl.BlockSpec(memory_space=pltpu.HBM)
    blocks = pl.pallas_call(
        pre_kernel,
        out_shape=jax.ShapeDtypeStruct((CHUNKS * SENT, FRAMES), jnp.float32),
        in_specs=[apart, apart],
        out_specs=whole,
        scratch_shapes=[
            pltpu.VMEM((3, FRAMES, ATOMS), jnp.float32),
            pltpu.VMEM((3, FRAMES, ATOMS), jnp.int32),
            pltpu.SemaphoreType.DMA((3 * PIECES * 2,)),
        ],
        compiler_params=params,
    )(jnp.transpose(wrapped, (1, 0, 2)), jnp.transpose(crossings, (1, 0, 2)))
    mine = lax.all_to_all(
        blocks.reshape(CHUNKS * SENT, 1, FRAMES), "tm", split_axis=0, concat_axis=0, tiled=True
    )
    return pl.pallas_call(
        post_kernel,
        out_shape=jax.ShapeDtypeStruct((4, LAGS), jnp.float32),
        in_specs=[whole, whole, whole, pl.BlockSpec(memory_space=pltpu.SMEM)],
        out_specs=whole,
        scratch_shapes=[pltpu.VMEM((CHUNKS * ROWS, 128), jnp.float32)] * 3,
        compiler_params=params,
    )(
        mine.reshape(CHUNKS * SENT, FRAMES),
        jnp.asarray(forward),
        jnp.asarray(backward),
        box_size,
    )


def solution(mesh):
    in_specs = (P("tm", None, None), P("tm", None, None), P())
    return jax.shard_map(
        on_device, mesh=mesh, in_specs=in_specs, out_specs=P("tm", None), check_vma=False
    )
```

```python
import jax
import jax.numpy as jnp
import numpy as np
from jax import lax
from jax.experimental import pallas as pl
from jax.experimental.pallas import tpu as pltpu
from jax.sharding import PartitionSpec as P

LAGS = 128
FRAMES = 128
CHUNKS = 128
ATOMS = 512
SENT = 13
ROWS = 16
PIECES = 2
VMEM = 48 * 1024 * 1024


def split(x):
    high = x.astype(jnp.bfloat16)
    low = (x - high.astype(x.dtype)).astype(jnp.bfloat16)
    return high, low


def tables():
    t = np.arange(FRAMES)[:, None].astype(np.float64)
    f = np.arange(FRAMES)[None, :].astype(np.float64)
    angle = 2.0 * np.pi * t * (f + 0.5) / 256.0
    forward = np.concatenate([np.cos(angle), -np.sin(angle)], axis=1)
    high, low = split(forward)
    forward = np.concatenate([high, high, low])

    turn = angle.T
    weight = 2.0 / 256.0
    sign = (1.0 - 2.0 * (np.arange(128) % 2))[:, None]
    same = 2.0 * weight * (1.0 - np.cos(turn))
    real = -2.0 * weight * sign * np.sin(turn)
    imag = -2.0 * weight * sign * np.cos(turn)
    j = np.arange(128)[:, None]
    k = np.arange(128)[None, :]
    head = (j < k).astype(np.float64)
    tail = (j > 127 - k).astype(np.float64)
    high, low = split(np.concatenate([same, real, imag, head, tail]))
    return forward, np.concatenate([high, low[:384]])


def pre_kernel(wrapped_hbm, crossings_hbm, out_ref, wrapped_ref, crossings_ref, sems):
    copies = []
    for c in range(3):
        for p in range(PIECES):
            rows = pl.ds(p * (FRAMES // PIECES), FRAMES // PIECES)
            for which, (src, dst) in enumerate(
                ((crossings_hbm, crossings_ref), (wrapped_hbm, wrapped_ref))
            ):
                copy = pltpu.make_async_copy(
                    src.at[c, rows], dst.at[c, rows], sems.at[(c * PIECES + p) * 2 + which]
                )
                copy.start()
                copies.append(copy)
    row = lax.broadcasted_iota(jnp.int32, (FRAMES, FRAMES), 0)
    col = lax.broadcasted_iota(jnp.int32, (FRAMES, FRAMES), 1)
    lower = jnp.where(col <= row, 1.0, 0.0).astype(jnp.bfloat16)
    own = lax.broadcasted_iota(jnp.int32, (4, ATOMS), 1) % 4 == lax.broadcasted_iota(
        jnp.int32, (4, ATOMS), 0
    )
    means, ends = [], []
    for c in range(3):
        for copy in copies[c * 2 * PIECES : (c + 1) * 2 * PIECES]:
            copy.wait()
        steps = crossings_ref[c].astype(jnp.float32).astype(jnp.bfloat16)
        counts = jnp.dot(lower, steps, preferred_element_type=jnp.float32)
        value = wrapped_ref[c] + counts
        mean = jnp.sum(value, axis=0, keepdims=True) * (1.0 / FRAMES)
        turned = (value - mean).T
        for d in range(CHUNKS):
            out_ref[SENT * d + 4 * c : SENT * d + 4 * c + 4, :] = turned[4 * d : 4 * d + 4]
        means.append(jnp.where(own, mean, 0.0))
        ends.append(jnp.where(own, counts[FRAMES - 1 : FRAMES] - mean, 0.0))
    blank = jnp.zeros((4, ATOMS), jnp.float32)
    notes = jnp.concatenate(means + [blank] + ends + [blank] * 25, axis=0)
    pick = jnp.where(
        lax.broadcasted_iota(jnp.int32, (CHUNKS, ATOMS), 1) // 4
        == lax.broadcasted_iota(jnp.int32, (CHUNKS, ATOMS), 0),
        1.0,
        0.0,
    ).astype(jnp.bfloat16)
    sent = jnp.zeros((CHUNKS, 128), jnp.float32)
    for _ in range(3):
        top = notes.astype(jnp.bfloat16)
        notes = notes - top.astype(jnp.float32)
        sent = sent + lax.dot_general(
            pick, top, (((1,), (1,)), ((), ())), preferred_element_type=jnp.float32
        )
    out_ref[pl.ds(SENT - 1, CHUNKS, stride=SENT), :] = sent


def post_kernel(
    x_ref, forward_ref, back_ref, box_hbm, out_ref, wide_ref, real_ref, imag_ref, box_ref, sem
):
    box_copy = pltpu.make_async_copy(box_hbm, box_ref, sem)
    box_copy.start()
    here = x_ref[pl.ds(SENT - 1, CHUNKS, stride=SENT), :]
    after = x_ref[pl.ds(2 * SENT - 1, CHUNKS - 1, stride=SENT), :]
    after = jnp.concatenate([after, jnp.zeros((1, 128), jnp.float32)], axis=0)
    ends = jnp.concatenate([here[:, 16:], here[:, :16]], axis=1)
    chunk = lax.broadcasted_iota(jnp.int32, (CHUNKS, 128), 0)
    gaps = jnp.where(chunk < CHUNKS - 1, after + ends, 0.0).T[0:ROWS]

    for d in range(CHUNKS):
        rows = ROWS if d < CHUNKS - 1 else SENT
        wide_ref[ROWS * d : ROWS * d + rows, :] = x_ref[SENT * d : SENT * d + rows, :]
    wide_ref[ROWS * CHUNKS - 3 : ROWS * CHUNKS, :] = jnp.zeros((3, 128), jnp.float32)
    for g in range(8):
        rows = slice(256 * g, 256 * g + 256)
        top, rest = split(wide_ref[rows, :])
        spec = jnp.dot(
            jnp.concatenate([top, rest, top], axis=1),
            forward_ref[...],
            preferred_element_type=jnp.float32,
        )
        real_ref[rows, :] = spec[:, :128]
        imag_ref[rows, :] = spec[:, 128:]

    zero = jnp.zeros((ROWS, 128), jnp.float32)
    same = both_r = both_i = za = zb = zero
    block = slice(0, ROWS)
    here_r, here_i, here_x = real_ref[block, :], imag_ref[block, :], wide_ref[block, :]
    for d in range(CHUNKS):
        same = same + (here_r * here_r + here_i * here_i)
        if d == CHUNKS - 1:
            break
        block = slice(ROWS * (d + 1), ROWS * (d + 2))
        next_r, next_i, next_x = real_ref[block, :], imag_ref[block, :], wide_ref[block, :]
        both_r = both_r + (here_r * next_r + here_i * next_i)
        both_i = both_i + (here_r * next_i - here_i * next_r)
        gap = jnp.broadcast_to(gaps[:, d : d + 1], (ROWS, 128))
        za = za + gap * here_x
        zb = zb + gap * next_x
        here_r, here_i, here_x = next_r, next_i, next_x
    first_x = wide_ref[0:ROWS, :]

    parts = jnp.concatenate(
        [
            same,
            both_r,
            both_i,
            2.0 * zb - first_x * first_x,
            -2.0 * za - here_x * here_x,
        ],
        axis=1,
    )
    top, rest = split(parts)
    sums = jnp.dot(top, back_ref[0:640, :], preferred_element_type=jnp.float32)
    sums += jnp.dot(rest, back_ref[0:640, :], preferred_element_type=jnp.float32)
    sums += jnp.dot(top[:, :384], back_ref[640:1024, :], preferred_element_type=jnp.float32)
    lags = lax.broadcasted_iota(jnp.int32, (ROWS, 128), 1).astype(jnp.float32)
    sums = sums + jnp.sum(gaps * gaps, axis=1, keepdims=True) * lags
    box_copy.wait()
    total = jnp.zeros((4, 128), jnp.float32)
    for c in range(3):
        total = total + sums[4 * c : 4 * c + 4] * (box_ref[c] * box_ref[c])
    out_ref[...] = total / (FRAMES * CHUNKS - lags[0:4])


def in_hbm(x):
    return pltpu.with_memory_space_constraint(x, pltpu.HBM)


def on_device(wrapped, crossings, box_size):
    forward, backward = tables()
    params = pltpu.CompilerParams(vmem_limit_bytes=VMEM)
    whole = pl.BlockSpec(memory_space=pltpu.VMEM)
    apart = pl.BlockSpec(memory_space=pltpu.HBM)
    blocks = pl.pallas_call(
        pre_kernel,
        out_shape=jax.ShapeDtypeStruct((CHUNKS * SENT, FRAMES), jnp.float32),
        in_specs=[apart, apart],
        out_specs=whole,
        scratch_shapes=[
            pltpu.VMEM((3, FRAMES, ATOMS), jnp.float32),
            pltpu.VMEM((3, FRAMES, ATOMS), jnp.int32),
            pltpu.SemaphoreType.DMA((3 * PIECES * 2,)),
        ],
        compiler_params=params,
    )(in_hbm(jnp.transpose(wrapped, (1, 0, 2))), in_hbm(jnp.transpose(crossings, (1, 0, 2))))
    mine = lax.all_to_all(
        blocks.reshape(CHUNKS * SENT, 1, FRAMES), "tm", split_axis=0, concat_axis=0, tiled=True
    )
    return pl.pallas_call(
        post_kernel,
        out_shape=jax.ShapeDtypeStruct((4, LAGS), jnp.float32),
        in_specs=[whole, whole, whole, apart],
        out_specs=whole,
        scratch_shapes=[pltpu.VMEM((CHUNKS * ROWS, 128), jnp.float32)] * 3
        + [pltpu.SMEM((3,), jnp.float32), pltpu.SemaphoreType.DMA],
        compiler_params=params,
    )(
        mine.reshape(CHUNKS * SENT, FRAMES),
        jnp.asarray(forward),
        jnp.asarray(backward),
        in_hbm(box_size),
    )


def solution(mesh):
    in_specs = (P("tm", None, None), P("tm", None, None), P())
    return jax.shard_map(
        on_device, mesh=mesh, in_specs=in_specs, out_specs=P("tm", None), check_vma=False
    )
```

```python
import jax
import jax.numpy as jnp
import numpy as np
from jax import lax
from jax.experimental import pallas as pl
from jax.experimental.pallas import tpu as pltpu
from jax.sharding import PartitionSpec as P

LAGS = 128
FRAMES = 128
CHUNKS = 128
ATOMS = 512
SENT = 13
ROWS = 16
VMEM = 48 * 1024 * 1024
ORDER = [d for j in range(CHUNKS // 2) for d in (CHUNKS - 1 - j, j)]
PLACE = [ORDER.index(d) for d in range(CHUNKS)]


def split(x):
    high = x.astype(jnp.bfloat16)
    low = (x - high.astype(x.dtype)).astype(jnp.bfloat16)
    return high, low


def tables():
    t = np.arange(FRAMES)[:, None].astype(np.float64)
    f = np.arange(FRAMES)[None, :].astype(np.float64)
    angle = 2.0 * np.pi * t * (f + 0.5) / 256.0
    forward = np.concatenate([np.cos(angle), -np.sin(angle)], axis=1)
    high, low = split(forward)
    forward = np.concatenate([high, high, low])

    turn = angle.T
    weight = 2.0 / 256.0
    sign = (1.0 - 2.0 * (np.arange(128) % 2))[:, None]
    same = 2.0 * weight * (1.0 - np.cos(turn))
    real = -2.0 * weight * sign * np.sin(turn)
    imag = -2.0 * weight * sign * np.cos(turn)
    j = np.arange(128)[:, None]
    k = np.arange(128)[None, :]
    head = (j < k).astype(np.float64)
    tail = (j > 127 - k).astype(np.float64)
    high, low = split(np.concatenate([same, real, imag, head, tail]))
    return forward, np.concatenate([high, low[:384]])


def pre_kernel(wrapped_hbm, crossings_hbm, out_ref, wrapped_ref, crossings_ref, sems):
    copies = []
    for c in range(3):
        for src, dst in ((crossings_hbm, crossings_ref), (wrapped_hbm, wrapped_ref)):
            copy = pltpu.make_async_copy(src.at[c], dst.at[c], sems.at[len(copies)])
            copy.start()
            copies.append(copy)
    row = lax.broadcasted_iota(jnp.int32, (FRAMES, FRAMES), 0)
    col = lax.broadcasted_iota(jnp.int32, (FRAMES, FRAMES), 1)
    upper = jnp.where(row <= col, 1.0, 0.0).astype(jnp.bfloat16)
    own = lax.broadcasted_iota(jnp.int32, (4, ATOMS), 1) % 4 == lax.broadcasted_iota(
        jnp.int32, (4, ATOMS), 0
    )
    place = lax.broadcasted_iota(jnp.int32, (CHUNKS, ATOMS), 0)
    owner = jnp.where(place % 2 == 0, CHUNKS - 1 - place // 2, place // 2)
    pick = jnp.where(
        lax.broadcasted_iota(jnp.int32, (CHUNKS, ATOMS), 1) // 4 == owner, 1.0, 0.0
    ).astype(jnp.bfloat16)
    means, ends = [], []
    for c in range(3):
        for copy in copies[2 * c : 2 * c + 2]:
            copy.wait()
        steps = crossings_ref[c].astype(jnp.float32).astype(jnp.bfloat16)
        moves = crossings_ref[c].astype(jnp.float32)
        left = (FRAMES - lax.broadcasted_iota(jnp.int32, (FRAMES, 1), 0)).astype(jnp.float32)
        mean = jnp.sum(wrapped_ref[c] + moves * left, axis=0, keepdims=True) * (1.0 / FRAMES)
        end = jnp.sum(moves, axis=0, keepdims=True)
        turned = (wrapped_ref[c] - mean).T + lax.dot_general(
            steps, upper, (((0,), (0,)), ((), ())), preferred_element_type=jnp.float32
        )
        for d in range(CHUNKS):
            start = SENT * PLACE[d] + 4 * c
            out_ref[start : start + 4, :] = turned[4 * d : 4 * d + 4]
        means.append(jnp.where(own, mean, 0.0))
        ends.append(jnp.where(own, end - mean, 0.0))
    blank = jnp.zeros((4, ATOMS), jnp.float32)
    notes = jnp.concatenate(means + [blank] + ends + [blank] * 25, axis=0)
    sent = jnp.zeros((CHUNKS, 128), jnp.float32)
    for _ in range(3):
        top = notes.astype(jnp.bfloat16)
        notes = notes - top.astype(jnp.float32)
        sent = sent + lax.dot_general(
            pick, top, (((1,), (1,)), ((), ())), preferred_element_type=jnp.float32
        )
    out_ref[pl.ds(SENT - 1, CHUNKS, stride=SENT), :] = sent


def post_kernel(
    x_ref, forward_ref, back_ref, box_hbm, out_ref, wide_ref, real_ref, imag_ref, box_ref, sem
):
    box_copy = pltpu.make_async_copy(box_hbm, box_ref, sem)
    box_copy.start()
    for d in range(CHUNKS):
        rows = ROWS if PLACE[d] < CHUNKS - 1 else SENT
        start = SENT * PLACE[d]
        wide_ref[ROWS * d : ROWS * d + rows, :] = x_ref[start : start + rows, :]
        if rows < ROWS:
            wide_ref[ROWS * d + rows : ROWS * d + ROWS, :] = jnp.zeros((ROWS - rows, 128), jnp.float32)

    here = wide_ref[pl.ds(SENT - 1, CHUNKS, stride=ROWS), :]
    after = wide_ref[pl.ds(ROWS + SENT - 1, CHUNKS - 1, stride=ROWS), :]
    after = jnp.concatenate([after, jnp.zeros((1, 128), jnp.float32)], axis=0)
    ends = jnp.concatenate([here[:, 16:], here[:, :16]], axis=1)
    chunk = lax.broadcasted_iota(jnp.int32, (CHUNKS, 128), 0)
    gaps = jnp.where(chunk < CHUNKS - 1, after + ends, 0.0).T[0:ROWS]

    for g in range(8):
        rows = slice(256 * g, 256 * g + 256)
        top, rest = split(wide_ref[rows, :])
        spec = jnp.dot(
            jnp.concatenate([top, rest, top], axis=1),
            forward_ref[...],
            preferred_element_type=jnp.float32,
        )
        real_ref[rows, :] = spec[:, :128]
        imag_ref[rows, :] = spec[:, 128:]

    zero = jnp.zeros((ROWS, 128), jnp.float32)
    same = both_r = both_i = za = zb = zero
    block = slice(0, ROWS)
    here_r, here_i, here_x = real_ref[block, :], imag_ref[block, :], wide_ref[block, :]
    for d in range(CHUNKS):
        same = same + (here_r * here_r + here_i * here_i)
        if d == CHUNKS - 1:
            break
        block = slice(ROWS * (d + 1), ROWS * (d + 2))
        next_r, next_i, next_x = real_ref[block, :], imag_ref[block, :], wide_ref[block, :]
        both_r = both_r + (here_r * next_r + here_i * next_i)
        both_i = both_i + (here_r * next_i - here_i * next_r)
        gap = jnp.broadcast_to(gaps[:, d : d + 1], (ROWS, 128))
        za = za + gap * here_x
        zb = zb + gap * next_x
        here_r, here_i, here_x = next_r, next_i, next_x
    first_x = wide_ref[0:ROWS, :]

    parts = jnp.concatenate(
        [
            same,
            both_r,
            both_i,
            2.0 * zb - first_x * first_x,
            -2.0 * za - here_x * here_x,
        ],
        axis=1,
    )
    top, rest = split(parts)
    sums = jnp.dot(top, back_ref[0:640, :], preferred_element_type=jnp.float32)
    sums += jnp.dot(rest, back_ref[0:640, :], preferred_element_type=jnp.float32)
    sums += jnp.dot(top[:, :384], back_ref[640:1024, :], preferred_element_type=jnp.float32)
    lags = lax.broadcasted_iota(jnp.int32, (ROWS, 128), 1).astype(jnp.float32)
    sums = sums + jnp.sum(gaps * gaps, axis=1, keepdims=True) * lags
    box_copy.wait()
    total = jnp.zeros((4, 128), jnp.float32)
    for c in range(3):
        total = total + sums[4 * c : 4 * c + 4] * (box_ref[c] * box_ref[c])
    out_ref[...] = total / (FRAMES * CHUNKS - lags[0:4])


def in_hbm(x):
    return pltpu.with_memory_space_constraint(x, pltpu.HBM)


def on_device(wrapped, crossings, box_size):
    forward, backward = tables()
    params = pltpu.CompilerParams(vmem_limit_bytes=VMEM)
    whole = pl.BlockSpec(memory_space=pltpu.VMEM)
    apart = pl.BlockSpec(memory_space=pltpu.HBM)
    blocks = pl.pallas_call(
        pre_kernel,
        out_shape=jax.ShapeDtypeStruct((CHUNKS * SENT, FRAMES), jnp.float32),
        in_specs=[apart, apart],
        out_specs=whole,
        scratch_shapes=[
            pltpu.VMEM((3, FRAMES, ATOMS), jnp.float32),
            pltpu.VMEM((3, FRAMES, ATOMS), jnp.int32),
            pltpu.SemaphoreType.DMA((6,)),
        ],
        compiler_params=params,
    )(in_hbm(jnp.transpose(wrapped, (1, 0, 2))), in_hbm(jnp.transpose(crossings, (1, 0, 2))))
    mine = lax.all_to_all(
        blocks.reshape(CHUNKS * SENT, 1, FRAMES),
        "tm",
        split_axis=0,
        concat_axis=0,
        tiled=True,
        axis_index_groups=[ORDER],
    )
    return pl.pallas_call(
        post_kernel,
        out_shape=jax.ShapeDtypeStruct((4, LAGS), jnp.float32),
        in_specs=[whole, whole, whole, apart],
        out_specs=whole,
        scratch_shapes=[pltpu.VMEM((CHUNKS * ROWS, 128), jnp.float32)] * 3
        + [pltpu.SMEM((3,), jnp.float32), pltpu.SemaphoreType.DMA],
        compiler_params=params,
    )(
        mine.reshape(CHUNKS * SENT, FRAMES),
        jnp.asarray(forward),
        jnp.asarray(backward),
        in_hbm(box_size),
    )


def solution(mesh):
    in_specs = (P("tm", None, None), P("tm", None, None), P())
    return jax.shard_map(
        on_device, mesh=mesh, in_specs=in_specs, out_specs=P("tm", None), check_vma=False
    )
```

```python
import jax
import jax.numpy as jnp
import numpy as np
from jax import lax
from jax.experimental import pallas as pl
from jax.experimental.pallas import tpu as pltpu
from jax.sharding import PartitionSpec as P

LAGS = 128
FRAMES = 128
CHUNKS = 128
ATOMS = 512
SENT = 13
ROWS = 16
VMEM = 48 * 1024 * 1024
ORDER = [d for j in range(CHUNKS // 2) for d in (CHUNKS - 1 - j, j ^ 1)]
PLACE = [ORDER.index(d) for d in range(CHUNKS)]


def split(x):
    high = x.astype(jnp.bfloat16)
    low = (x - high.astype(x.dtype)).astype(jnp.bfloat16)
    return high, low


def tables():
    t = np.arange(FRAMES)[:, None].astype(np.float64)
    f = np.arange(FRAMES)[None, :].astype(np.float64)
    angle = 2.0 * np.pi * t * (f + 0.5) / 256.0
    forward = np.concatenate([np.cos(angle), -np.sin(angle)], axis=1)
    high, low = split(forward)
    forward = np.concatenate([high, high, low])

    turn = angle.T
    weight = 2.0 / 256.0
    sign = (1.0 - 2.0 * (np.arange(128) % 2))[:, None]
    same = 2.0 * weight * (1.0 - np.cos(turn))
    real = -2.0 * weight * sign * np.sin(turn)
    imag = -2.0 * weight * sign * np.cos(turn)
    j = np.arange(128)[:, None]
    k = np.arange(128)[None, :]
    head = (j < k).astype(np.float64)
    tail = (j > 127 - k).astype(np.float64)
    high, low = split(np.concatenate([same, real, imag, head, tail]))
    return forward, np.concatenate([high, low[:384]])


def pre_kernel(wrapped_hbm, crossings_hbm, out_ref, wrapped_ref, crossings_ref, sems):
    copies = []
    for c in range(3):
        for src, dst in ((crossings_hbm, crossings_ref), (wrapped_hbm, wrapped_ref)):
            copy = pltpu.make_async_copy(src.at[c], dst.at[c], sems.at[len(copies)])
            copy.start()
            copies.append(copy)
    row = lax.broadcasted_iota(jnp.int32, (FRAMES, FRAMES), 0)
    col = lax.broadcasted_iota(jnp.int32, (FRAMES, FRAMES), 1)
    upper = jnp.where(row <= col, 1.0, 0.0).astype(jnp.bfloat16)
    own = lax.broadcasted_iota(jnp.int32, (4, ATOMS), 1) % 4 == lax.broadcasted_iota(
        jnp.int32, (4, ATOMS), 0
    )
    place = lax.broadcasted_iota(jnp.int32, (CHUNKS, ATOMS), 0)
    pair = place // 2
    owner = jnp.where(place % 2 == 0, CHUNKS - 1 - pair, pair + 1 - 2 * (pair % 2))
    pick = jnp.where(
        lax.broadcasted_iota(jnp.int32, (CHUNKS, ATOMS), 1) // 4 == owner, 1.0, 0.0
    ).astype(jnp.bfloat16)
    means, ends = [], []
    for c in range(3):
        for copy in copies[2 * c : 2 * c + 2]:
            copy.wait()
        steps = crossings_ref[c].astype(jnp.float32).astype(jnp.bfloat16)
        moves = crossings_ref[c].astype(jnp.float32)
        left = (FRAMES - lax.broadcasted_iota(jnp.int32, (FRAMES, 1), 0)).astype(jnp.float32)
        mean = jnp.sum(wrapped_ref[c] + moves * left, axis=0, keepdims=True) * (1.0 / FRAMES)
        end = jnp.sum(moves, axis=0, keepdims=True)
        turned = (wrapped_ref[c] - mean).T + lax.dot_general(
            steps, upper, (((0,), (0,)), ((), ())), preferred_element_type=jnp.float32
        )
        for d in range(CHUNKS):
            start = SENT * PLACE[d] + 4 * c
            out_ref[start : start + 4, :] = turned[4 * d : 4 * d + 4]
        means.append(jnp.where(own, mean, 0.0))
        ends.append(jnp.where(own, end - mean, 0.0))
    blank = jnp.zeros((4, ATOMS), jnp.float32)
    notes = jnp.concatenate(means + [blank] + ends + [blank] * 25, axis=0)
    sent = jnp.zeros((CHUNKS, 128), jnp.float32)
    for _ in range(3):
        top = notes.astype(jnp.bfloat16)
        notes = notes - top.astype(jnp.float32)
        sent = sent + lax.dot_general(
            pick, top, (((1,), (1,)), ((), ())), preferred_element_type=jnp.float32
        )
    out_ref[pl.ds(SENT - 1, CHUNKS, stride=SENT), :] = sent


def post_kernel(
    x_ref, forward_ref, back_ref, box_hbm, out_ref, wide_ref, real_ref, imag_ref, box_ref, sem
):
    box_copy = pltpu.make_async_copy(box_hbm, box_ref, sem)
    box_copy.start()
    for d in range(CHUNKS):
        rows = ROWS if PLACE[d] < CHUNKS - 1 else SENT
        start = SENT * PLACE[d]
        wide_ref[ROWS * d : ROWS * d + rows, :] = x_ref[start : start + rows, :]
        if rows < ROWS:
            wide_ref[ROWS * d + rows : ROWS * d + ROWS, :] = jnp.zeros((ROWS - rows, 128), jnp.float32)

    here = wide_ref[pl.ds(SENT - 1, CHUNKS, stride=ROWS), :]
    after = wide_ref[pl.ds(ROWS + SENT - 1, CHUNKS - 1, stride=ROWS), :]
    after = jnp.concatenate([after, jnp.zeros((1, 128), jnp.float32)], axis=0)
    ends = jnp.concatenate([here[:, 16:], here[:, :16]], axis=1)
    chunk = lax.broadcasted_iota(jnp.int32, (CHUNKS, 128), 0)
    gaps = jnp.where(chunk < CHUNKS - 1, after + ends, 0.0).T[0:ROWS]

    for g in range(8):
        rows = slice(256 * g, 256 * g + 256)
        top, rest = split(wide_ref[rows, :])
        spec = jnp.dot(
            jnp.concatenate([top, rest, top], axis=1),
            forward_ref[...],
            preferred_element_type=jnp.float32,
        )
        real_ref[rows, :] = spec[:, :128]
        imag_ref[rows, :] = spec[:, 128:]

    zero = jnp.zeros((ROWS, 128), jnp.float32)
    same = both_r = both_i = za = zb = zero
    block = slice(0, ROWS)
    here_r, here_i, here_x = real_ref[block, :], imag_ref[block, :], wide_ref[block, :]
    for d in range(CHUNKS):
        same = same + (here_r * here_r + here_i * here_i)
        if d == CHUNKS - 1:
            break
        block = slice(ROWS * (d + 1), ROWS * (d + 2))
        next_r, next_i, next_x = real_ref[block, :], imag_ref[block, :], wide_ref[block, :]
        both_r = both_r + (here_r * next_r + here_i * next_i)
        both_i = both_i + (here_r * next_i - here_i * next_r)
        gap = jnp.broadcast_to(gaps[:, d : d + 1], (ROWS, 128))
        za = za + gap * here_x
        zb = zb + gap * next_x
        here_r, here_i, here_x = next_r, next_i, next_x
    first_x = wide_ref[0:ROWS, :]

    parts = jnp.concatenate(
        [
            same,
            both_r,
            both_i,
            2.0 * zb - first_x * first_x,
            -2.0 * za - here_x * here_x,
        ],
        axis=1,
    )
    top, rest = split(parts)
    sums = jnp.dot(top, back_ref[0:640, :], preferred_element_type=jnp.float32)
    sums += jnp.dot(rest, back_ref[0:640, :], preferred_element_type=jnp.float32)
    sums += jnp.dot(top[:, :384], back_ref[640:1024, :], preferred_element_type=jnp.float32)
    lags = lax.broadcasted_iota(jnp.int32, (ROWS, 128), 1).astype(jnp.float32)
    sums = sums + jnp.sum(gaps * gaps, axis=1, keepdims=True) * lags
    box_copy.wait()
    total = jnp.zeros((4, 128), jnp.float32)
    for c in range(3):
        total = total + sums[4 * c : 4 * c + 4] * (box_ref[c] * box_ref[c])
    out_ref[...] = total / (FRAMES * CHUNKS - lags[0:4])


def in_hbm(x):
    return pltpu.with_memory_space_constraint(x, pltpu.HBM)


def on_device(wrapped, crossings, box_size):
    forward, backward = tables()
    params = pltpu.CompilerParams(vmem_limit_bytes=VMEM)
    whole = pl.BlockSpec(memory_space=pltpu.VMEM)
    apart = pl.BlockSpec(memory_space=pltpu.HBM)
    blocks = pl.pallas_call(
        pre_kernel,
        out_shape=jax.ShapeDtypeStruct((CHUNKS * SENT, FRAMES), jnp.float32),
        in_specs=[apart, apart],
        out_specs=whole,
        scratch_shapes=[
            pltpu.VMEM((3, FRAMES, ATOMS), jnp.float32),
            pltpu.VMEM((3, FRAMES, ATOMS), jnp.int32),
            pltpu.SemaphoreType.DMA((6,)),
        ],
        compiler_params=params,
    )(in_hbm(jnp.transpose(wrapped, (1, 0, 2))), in_hbm(jnp.transpose(crossings, (1, 0, 2))))
    mine = lax.all_to_all(
        blocks.reshape(CHUNKS * SENT, 1, FRAMES),
        "tm",
        split_axis=0,
        concat_axis=0,
        tiled=True,
        axis_index_groups=[ORDER],
    )
    return pl.pallas_call(
        post_kernel,
        out_shape=jax.ShapeDtypeStruct((4, LAGS), jnp.float32),
        in_specs=[whole, whole, whole, apart],
        out_specs=whole,
        scratch_shapes=[pltpu.VMEM((CHUNKS * ROWS, 128), jnp.float32)] * 3
        + [pltpu.SMEM((3,), jnp.float32), pltpu.SemaphoreType.DMA],
        compiler_params=params,
    )(
        mine.reshape(CHUNKS * SENT, FRAMES),
        jnp.asarray(forward),
        jnp.asarray(backward),
        in_hbm(box_size),
    )


def solution(mesh):
    in_specs = (P("tm", None, None), P("tm", None, None), P())
    return jax.shard_map(
        on_device, mesh=mesh, in_specs=in_specs, out_specs=P("tm", None), check_vma=False
    )
```

```python
import jax
import jax.numpy as jnp
import numpy as np
from jax import lax
from jax.experimental import pallas as pl
from jax.experimental.pallas import tpu as pltpu
from jax.sharding import PartitionSpec as P

LAGS = 128
FRAMES = 128
CHUNKS = 128
ATOMS = 512
SENT = 13
ROWS = 16
VMEM = 48 * 1024 * 1024
ORDER = [d for j in range(CHUNKS // 2) for d in (CHUNKS - 1 - j, j ^ 1)]
PLACE = [ORDER.index(d) for d in range(CHUNKS)]


def split(x):
    high = x.astype(jnp.bfloat16)
    low = (x - high.astype(x.dtype)).astype(jnp.bfloat16)
    return high, low


def tables():
    t = np.arange(FRAMES)[:, None].astype(np.float64)
    f = np.arange(FRAMES)[None, :].astype(np.float64)
    angle = 2.0 * np.pi * t * (f + 0.5) / 256.0
    forward = np.concatenate([np.cos(angle), -np.sin(angle)], axis=1)
    high, low = split(forward)
    forward = np.concatenate([high, high, low])

    turn = angle.T
    weight = 2.0 / 256.0
    sign = (1.0 - 2.0 * (np.arange(128) % 2))[:, None]
    same = 2.0 * weight * (1.0 - np.cos(turn))
    real = -2.0 * weight * sign * np.sin(turn)
    imag = -2.0 * weight * sign * np.cos(turn)
    j = np.arange(128)[:, None]
    k = np.arange(128)[None, :]
    head = (j < k).astype(np.float64)
    tail = (j > 127 - k).astype(np.float64)
    high, low = split(np.concatenate([same, real, imag, head, tail]))
    return forward, np.concatenate([high, low[:384]])


def pre_kernel(wrapped_hbm, crossings_hbm, out_ref, wrapped_ref, crossings_ref, sems):
    copies = []
    for c in range(3):
        for src, dst in ((crossings_hbm, crossings_ref), (wrapped_hbm, wrapped_ref)):
            copy = pltpu.make_async_copy(src.at[c], dst.at[c], sems.at[len(copies)])
            copy.start()
            copies.append(copy)
    row = lax.broadcasted_iota(jnp.int32, (FRAMES, FRAMES), 0)
    col = lax.broadcasted_iota(jnp.int32, (FRAMES, FRAMES), 1)
    upper = jnp.where(row <= col, 1.0, 0.0).astype(jnp.bfloat16)
    own = lax.broadcasted_iota(jnp.int32, (4, ATOMS), 1) % 4 == lax.broadcasted_iota(
        jnp.int32, (4, ATOMS), 0
    )
    place = lax.broadcasted_iota(jnp.int32, (CHUNKS, ATOMS), 0)
    pair = place // 2
    owner = jnp.where(place % 2 == 0, CHUNKS - 1 - pair, pair + 1 - 2 * (pair % 2))
    pick = jnp.where(
        lax.broadcasted_iota(jnp.int32, (CHUNKS, ATOMS), 1) // 4 == owner, 1.0, 0.0
    ).astype(jnp.bfloat16)
    means, ends = [], []
    for copy in copies:
        copy.wait()
    for c in range(3):
        steps = crossings_ref[c].astype(jnp.float32).astype(jnp.bfloat16)
        moves = crossings_ref[c].astype(jnp.float32)
        left = (FRAMES - lax.broadcasted_iota(jnp.int32, (FRAMES, 1), 0)).astype(jnp.float32)
        mean = jnp.sum(wrapped_ref[c] + moves * left, axis=0, keepdims=True) * (1.0 / FRAMES)
        end = jnp.sum(moves, axis=0, keepdims=True)
        turned = (wrapped_ref[c] - mean).T + lax.dot_general(
            steps, upper, (((0,), (0,)), ((), ())), preferred_element_type=jnp.float32
        )
        for d in range(CHUNKS):
            start = SENT * PLACE[d] + 4 * c
            out_ref[start : start + 4, :] = turned[4 * d : 4 * d + 4]
        means.append(jnp.where(own, mean, 0.0))
        ends.append(jnp.where(own, end - mean, 0.0))
    blank = jnp.zeros((4, ATOMS), jnp.float32)
    notes = jnp.concatenate(means + [blank] + ends + [blank] * 25, axis=0)
    sent = jnp.zeros((CHUNKS, 128), jnp.float32)
    for _ in range(3):
        top = notes.astype(jnp.bfloat16)
        notes = notes - top.astype(jnp.float32)
        sent = sent + lax.dot_general(
            pick, top, (((1,), (1,)), ((), ())), preferred_element_type=jnp.float32
        )
    out_ref[pl.ds(SENT - 1, CHUNKS, stride=SENT), :] = sent


def post_kernel(
    x_ref, forward_ref, back_ref, box_hbm, out_ref, wide_ref, real_ref, imag_ref, box_ref, sem
):
    box_copy = pltpu.make_async_copy(box_hbm, box_ref, sem)
    box_copy.start()
    for d in range(CHUNKS):
        rows = ROWS if PLACE[d] < CHUNKS - 1 else SENT
        start = SENT * PLACE[d]
        wide_ref[ROWS * d : ROWS * d + rows, :] = x_ref[start : start + rows, :]
        if rows < ROWS:
            wide_ref[ROWS * d + rows : ROWS * d + ROWS, :] = jnp.zeros((ROWS - rows, 128), jnp.float32)

    here = wide_ref[pl.ds(SENT - 1, CHUNKS, stride=ROWS), :]
    after = wide_ref[pl.ds(ROWS + SENT - 1, CHUNKS - 1, stride=ROWS), :]
    after = jnp.concatenate([after, jnp.zeros((1, 128), jnp.float32)], axis=0)
    ends = jnp.concatenate([here[:, 16:], here[:, :16]], axis=1)
    chunk = lax.broadcasted_iota(jnp.int32, (CHUNKS, 128), 0)
    gaps = jnp.where(chunk < CHUNKS - 1, after + ends, 0.0).T[0:ROWS]

    for g in range(8):
        rows = slice(256 * g, 256 * g + 256)
        top, rest = split(wide_ref[rows, :])
        spec = jnp.dot(
            jnp.concatenate([top, rest, top], axis=1),
            forward_ref[...],
            preferred_element_type=jnp.float32,
        )
        real_ref[rows, :] = spec[:, :128]
        imag_ref[rows, :] = spec[:, 128:]

    zero = jnp.zeros((ROWS, 128), jnp.float32)
    same = both_r = both_i = za = zb = zero
    block = slice(0, ROWS)
    here_r, here_i, here_x = real_ref[block, :], imag_ref[block, :], wide_ref[block, :]
    for d in range(CHUNKS):
        same = same + (here_r * here_r + here_i * here_i)
        if d == CHUNKS - 1:
            break
        block = slice(ROWS * (d + 1), ROWS * (d + 2))
        next_r, next_i, next_x = real_ref[block, :], imag_ref[block, :], wide_ref[block, :]
        both_r = both_r + (here_r * next_r + here_i * next_i)
        both_i = both_i + (here_r * next_i - here_i * next_r)
        gap = jnp.broadcast_to(gaps[:, d : d + 1], (ROWS, 128))
        za = za + gap * here_x
        zb = zb + gap * next_x
        here_r, here_i, here_x = next_r, next_i, next_x
    first_x = wide_ref[0:ROWS, :]

    parts = jnp.concatenate(
        [
            same,
            both_r,
            both_i,
            2.0 * zb - first_x * first_x,
            -2.0 * za - here_x * here_x,
        ],
        axis=1,
    )
    top, rest = split(parts)
    sums = jnp.dot(top, back_ref[0:640, :], preferred_element_type=jnp.float32)
    sums += jnp.dot(rest, back_ref[0:640, :], preferred_element_type=jnp.float32)
    sums += jnp.dot(top[:, :384], back_ref[640:1024, :], preferred_element_type=jnp.float32)
    lags = lax.broadcasted_iota(jnp.int32, (ROWS, 128), 1).astype(jnp.float32)
    sums = sums + jnp.sum(gaps * gaps, axis=1, keepdims=True) * lags
    box_copy.wait()
    total = jnp.zeros((4, 128), jnp.float32)
    for c in range(3):
        total = total + sums[4 * c : 4 * c + 4] * (box_ref[c] * box_ref[c])
    out_ref[...] = total / (FRAMES * CHUNKS - lags[0:4])


def in_hbm(x):
    return pltpu.with_memory_space_constraint(x, pltpu.HBM)


def on_device(wrapped, crossings, box_size):
    forward, backward = tables()
    params = pltpu.CompilerParams(vmem_limit_bytes=VMEM)
    whole = pl.BlockSpec(memory_space=pltpu.VMEM)
    apart = pl.BlockSpec(memory_space=pltpu.HBM)
    blocks = pl.pallas_call(
        pre_kernel,
        out_shape=jax.ShapeDtypeStruct((CHUNKS * SENT, FRAMES), jnp.float32),
        in_specs=[apart, apart],
        out_specs=whole,
        scratch_shapes=[
            pltpu.VMEM((3, FRAMES, ATOMS), jnp.float32),
            pltpu.VMEM((3, FRAMES, ATOMS), jnp.int32),
            pltpu.SemaphoreType.DMA((6,)),
        ],
        compiler_params=params,
    )(in_hbm(jnp.transpose(wrapped, (1, 0, 2))), in_hbm(jnp.transpose(crossings, (1, 0, 2))))
    mine = lax.all_to_all(
        blocks.reshape(CHUNKS * SENT, 1, FRAMES),
        "tm",
        split_axis=0,
        concat_axis=0,
        tiled=True,
        axis_index_groups=[ORDER],
    )
    return pl.pallas_call(
        post_kernel,
        out_shape=jax.ShapeDtypeStruct((4, LAGS), jnp.float32),
        in_specs=[whole, whole, whole, apart],
        out_specs=whole,
        scratch_shapes=[pltpu.VMEM((CHUNKS * ROWS, 128), jnp.float32)] * 3
        + [pltpu.SMEM((3,), jnp.float32), pltpu.SemaphoreType.DMA],
        compiler_params=params,
    )(
        mine.reshape(CHUNKS * SENT, FRAMES),
        jnp.asarray(forward),
        jnp.asarray(backward),
        in_hbm(box_size),
    )


def solution(mesh):
    in_specs = (P("tm", None, None), P("tm", None, None), P())
    return jax.shard_map(
        on_device, mesh=mesh, in_specs=in_specs, out_specs=P("tm", None), check_vma=False
    )
```
